768 devices in a mesh: fsdp: 12 (over z_lo, core), dp: 64 (over x, z_hi, y).
Axes of the slice: x: 4, y: 8, z: 12 (z_hi: 2, z_lo: 6; z = z_hi * 6 + z_lo), core: 2. Of those that a mesh axis runs over, the one named last changes fastest.
Arguments:
- inputs: bfloat16 [98304, 8192], P(('fsdp', 'dp')), may hold values from -6 to 6
- cotangent: bfloat16 [98304, 7680], P(('fsdp', 'dp')), may hold values from -0.15625 to 0.15625
- projection_basis: bfloat16 [8192, 128], replicated, may hold values from -0.15625 to 0.15625
- first_moment: float32 [7680, 128], P('fsdp'), may hold values from -4 to 4
- second_moment: float32 [7680, 128], P('fsdp'), may hold values from 0.01 to 4
Outputs:
- first_new: float32 [7680, 128], P('fsdp')
- second_new: float32 [7680, 128], P('fsdp')
- update: float32 [7680, 8192], P('fsdp', 'dp')
The draws below stay inside these ranges and needn't reach their ends.
All inputs are finite; a program needn't handle non-finite values.
Results may differ from the reference program's by a relative error of at most 0.0014.
Values sent between devices are 32-bit elements; how exact they have to be, the bound alone decides.
No kernel may reach another device: no remote copies, remote signals or barrier semaphores. Data moves between devices by JAX's collectives and lax.ppermute only.
A program may use at most 32 MiB of HBM per device.

```python
import math
import jax
import jax.numpy as jnp
from jax import lax

IN = 8192
RANK = 128
TOK_DEV = 128
OUT = 7680
TOKENS = 98304


def strengthened(drawn, rng, source, target, blocks, factor):
    def block_of(dim):
        return (jnp.arange(drawn.shape[dim]) // (drawn.shape[dim] // blocks)).reshape((-1,) + (1,) * (drawn.ndim - 1 - dim))

    one_side = jax.random.permutation(rng, blocks)[block_of(target)]
    other_side = (block_of(target) + blocks // 2) % blocks
    return jnp.where((block_of(source) == one_side) | (block_of(source) == other_side), factor * drawn, drawn)


def shard_levels(stream_key, dims, cuts, low, top_value):
    level, own = 1.0, jax.random.fold_in(stream_key, 6)
    for dim, shards_of in cuts:
        draws = jnp.exp(jax.random.uniform(jax.random.fold_in(own, dim), (shards_of,), jnp.float32, low / len(cuts), top_value / len(cuts)))
        level = level * jnp.repeat(draws, dims[dim] // shards_of).reshape([-1 if axis == dim else 1 for axis in range(len(dims))])
    return level


def centred(own_key, shape, deviation, bound, cuts=(), kind=jnp.bfloat16):
    result = deviation * jax.random.normal(own_key, shape, jnp.float32)
    if cuts:
        result = result * shard_levels(own_key, shape, cuts, -0.22, 0.18)
    return jnp.clip(result, -bound, bound).astype(kind)


def heavy_noise(stream_key, shape, width, reach, pieces, heavy, dtype=jnp.bfloat16):
    array = width * jax.random.normal(stream_key, shape, jnp.float32)
    if pieces:
        array = array * shard_levels(stream_key, shape, pieces, -0.22, 0.18)
    return jnp.clip(strengthened(array, jax.random.fold_in(stream_key, 3), *heavy), -reach, reach).astype(dtype)


def setup_inputs(seed: int = 0) -> dict:
    streams_of = jax.random.split(jax.random.key(seed), 6)
    inputs = centred(streams_of[0], (TOKENS, IN), 1.0, 6.0, ((0, 768),))
    cotangent = heavy_noise(streams_of[1], (TOKENS, OUT), (2.0 * TOKENS ** -0.5), 0.15625, ((0, 768),), (0, 1, 768, 6.0))
    projection_basis = centred(streams_of[2], (IN, RANK), (IN ** -0.5), 0.15625)
    first_moment = centred(streams_of[3], (OUT, RANK), 0.5, 4.0, ((0, 12),), jnp.float32)
    second_moment = jnp.clip(jnp.exp(math.log(4.0) - 5.9914646 * jax.random.uniform(streams_of[4], (OUT, RANK), jnp.float32) ** shard_levels(streams_of[4], (OUT, RANK), ((0, 12),), -0.2, 0.2)), 0.01, 4.0)
    return {"inputs": inputs, "cotangent": cotangent, "projection_basis": projection_basis, "first_moment": first_moment, "second_moment": second_moment}


bias_first = 1.0 - 0.9 ** 10
bias_second = 1.0 - 0.999 ** 10

def reference(inputs, cotangent, projection_basis, first_moment, second_moment):
    block_count = TOKENS // TOK_DEV
    input_blocks = inputs.reshape(block_count, TOK_DEV, IN)
    grad_blocks = cotangent.reshape(block_count, TOK_DEV, OUT)

    def accumulate(running, tiles):
        input_tile, grad_tile = tiles
        projected = jnp.dot(input_tile, projection_basis, preferred_element_type=jnp.float32).astype(jnp.bfloat16)
        term = lax.dot_general(grad_tile, projected, (((0,), (0,)), ((), ())), preferred_element_type=jnp.float32)
        return (running + term, None)
    gradient, _ = lax.scan(accumulate, jnp.zeros((OUT, RANK), jnp.float32), (input_blocks, grad_blocks))
    first_new = 0.9 * first_moment + 0.1 * gradient
    second_new = 0.999 * second_moment + 0.001 * gradient * gradient
    direction = first_new / bias_first / (jnp.sqrt(second_new / bias_second) + 1e-08)
    update = 0.25 * jnp.dot(direction, projection_basis.astype(jnp.float32).T, precision=lax.Precision.HIGHEST)
    return (first_new, second_new, update)
```

```python
import jax
import jax.numpy as jnp
from jax import lax
from jax.experimental import pallas as pl
from jax.experimental.pallas import tpu as pltpu
from jax.sharding import PartitionSpec as P

bias_first = 1.0 - 0.9**10
bias_second = 1.0 - 0.999**10

AXES = ("fsdp", "dp")
X, Y, ZH, ZL = 4, 8, 2, 6
Z = ZH * ZL
IN, OUT, RANK, TOK = 8192, 7680, 128, 128
CHUNK = OUT // (2 * ZL)
COLS = IN // (X * ZH * Y)
KT = 4


def device(x, y, z, core):
    z_hi, z_lo = z // ZL, z % ZL
    return (((z_lo * 2 + core) * X + x) * ZH + z_hi) * Y + y


CORES = (0, 1)


def pairs(size, core):
    if core == 0:
        return [(i, i + 1) for i in range(0, size, 2)]
    return [((i + 1) % size, i) for i in range(1, size, 2)]


NEAR = [
    [device(x, y, z, c) for z in pz for x in px for y in py]
    for c in CORES
    for px in pairs(X, c)
    for py in pairs(Y, c)
    for pz in pairs(Z, c)
]
FAR = [
    [device(2 * i + a, 2 * j + b, z, c) for i in range(X // 2) for j in range(Y // 2)]
    for c in CORES
    for z in range(Z)
    for a in range(2)
    for b in range(2)
]
DEEP = [
    [device(x, y, 2 * i + p, c) for i in range(Z // 2)]
    for c in CORES
    for x in range(X)
    for y in range(Y)
    for p in range(2)
]
PLANE = [
    [
        device(2 * i + a, 2 * j + b, z, c)
        for a in range(2)
        for b in range(2)
        for i in range(X // 2)
        for j in range(Y // 2)
    ]
    for c in CORES
    for z in range(Z)
]
SWAP = [
    (device(x, y, z, c), device(x, y, z, 1 - c))
    for x in range(X)
    for y in range(Y)
    for z in range(Z)
    for c in CORES
]


def exchange(blocks, groups):
    return lax.all_to_all(blocks, AXES, 0, 0, axis_index_groups=groups, tiled=True)


def half_copies(c_hbm, c, half, sems):
    def copy(i):
        cols = pl.ds(pl.multiple_of((2 * i + half) * CHUNK, 128), CHUNK)
        return pltpu.make_async_copy(c_hbm.at[:, cols], c.at[i], sems.at[i])

    return [copy(i) for i in range(ZL)]


def half_gradient(turned, c, out):
    for i in range(ZL):
        grad = jnp.dot(turned, c[i], preferred_element_type=jnp.float32)
        out[i % 2, :, i // 2] = grad.reshape(4, RANK // 4, CHUNK)


def first_kernel(place, x_hbm, b_hbm, c_hbm, out, p_out, x, b, c, xs, bs, cs):
    width = IN // KT

    def x_copy(i):
        part = pl.ds(i * width, width)
        return pltpu.make_async_copy(x_hbm.at[:, part], x.at[:, part], xs.at[i])

    def b_copy(i):
        part = pl.ds(i * width, width)
        return pltpu.make_async_copy(b_hbm.at[part, :], b.at[part, :], bs.at[i])

    for i in range(KT):
        x_copy(i).start()
        b_copy(i).start()
    c_copies = half_copies(c_hbm, c, 1 - place[0], cs)
    for copy in c_copies:
        copy.start()
    total = jnp.zeros((TOK, RANK), jnp.float32)
    for i in range(KT):
        x_copy(i).wait()
        b_copy(i).wait()
        part = pl.ds(i * width, width)
        total += jnp.dot(x[:, part], b[part, :], preferred_element_type=jnp.float32)
    turned = total.T.astype(jnp.bfloat16)
    p_out[...] = turned
    for copy in c_copies:
        copy.wait()
    half_gradient(turned, c, out)


HALF = (2, 4, ZL // 2, RANK // 4, CHUNK)
SMEM = pl.BlockSpec(memory_space=pltpu.SMEM)
VMEM = pl.BlockSpec(memory_space=pltpu.VMEM)
HBM = pl.BlockSpec(memory_space=pltpu.HBM)


def in_hbm(array):
    return pltpu.with_memory_space_constraint(array, pltpu.HBM)


def in_vmem(array):
    return pltpu.with_memory_space_constraint(array, pltpu.VMEM)


def first(place, inputs, basis, cotangent):
    return pl.pallas_call(
        first_kernel,
        out_shape=(pltpu.VMEM(HALF, jnp.float32), pltpu.VMEM((RANK, TOK), jnp.bfloat16)),
        in_specs=[SMEM, HBM, HBM, HBM],
        out_specs=(VMEM, VMEM),
        scratch_shapes=[
            pltpu.VMEM((TOK, IN), jnp.bfloat16),
            pltpu.VMEM((IN, RANK), jnp.bfloat16),
            pltpu.VMEM((ZL, TOK, CHUNK), jnp.bfloat16),
            pltpu.SemaphoreType.DMA((KT,)),
            pltpu.SemaphoreType.DMA((KT,)),
            pltpu.SemaphoreType.DMA((ZL,)),
        ],
        compiler_params=pltpu.CompilerParams(vmem_limit_bytes=24 << 20),
        name="first",
    )(place, *map(in_hbm, (inputs, basis, cotangent)))


def own_kernel(place, turned, c_hbm, basis_hbm, m_hbm, v_hbm, out, cols, m, v, c, cs, sems):
    rows = pl.ds(pl.multiple_of(place[1] * COLS, COLS), COLS)
    copies = half_copies(c_hbm, c, place[0], cs) + [
        pltpu.make_async_copy(basis_hbm.at[rows, :], cols, sems.at[0]),
        pltpu.make_async_copy(m_hbm, m, sems.at[1]),
        pltpu.make_async_copy(v_hbm, v, sems.at[2]),
    ]
    for copy in copies:
        copy.start()
    for copy in copies:
        copy.wait()
    half_gradient(turned[...], c, out)


def own(place, turned, cotangent, basis, m, v):
    return pl.pallas_call(
        own_kernel,
        out_shape=(
            pltpu.VMEM(HALF, jnp.float32),
            pltpu.VMEM((COLS, RANK), jnp.bfloat16),
            pltpu.VMEM((CHUNK, RANK), jnp.float32),
            pltpu.VMEM((CHUNK, RANK), jnp.float32),
        ),
        in_specs=[SMEM, VMEM, HBM, HBM, HBM, HBM],
        out_specs=(VMEM,) * 4,
        scratch_shapes=[
            pltpu.VMEM((ZL, TOK, CHUNK), jnp.bfloat16),
            pltpu.SemaphoreType.DMA((ZL,)),
            pltpu.SemaphoreType.DMA((3,)),
        ],
        compiler_params=pltpu.CompilerParams(vmem_limit_bytes=24 << 20),
        cost_estimate=pl.CostEstimate(
            flops=TOK * RANK * OUT, bytes_accessed=TOK * OUT + 2 * RANK * OUT, transcendentals=0
        ),
        name="own",
    )(place, in_vmem(turned), *map(in_hbm, (cotangent, basis, m, v)))


def adam_step(gradient, first_moment, second_moment):
    first_new = 0.9 * first_moment + 0.1 * gradient
    second_new = 0.999 * second_moment + 0.001 * gradient * gradient
    direction = first_new / bias_first / (jnp.sqrt(second_new / bias_second) + 1e-08)
    return (first_new, second_new, direction)


def spread_kernel(deep, out):
    part = deep[0]
    for i in range(1, deep.shape[0]):
        part += deep[i]
    for i in range(out.shape[0]):
        out[i] = part


def spread(deep):
    return pl.pallas_call(
        spread_kernel,
        out_shape=pltpu.VMEM((X * Y,) + deep.shape[1:], jnp.float32),
        in_specs=[VMEM],
        out_specs=VMEM,
        name="spread",
    )(in_vmem(deep))


def last_kernel(parts, cols, m, v, m_hbm, v_hbm, up_hbm, turned, m_out, v_out, up_out, sems):
    copies = [
        pltpu.make_async_copy(m_out, m_hbm, sems.at[0]),
        pltpu.make_async_copy(v_out, v_hbm, sems.at[1]),
        pltpu.make_async_copy(up_out, up_hbm, sems.at[2]),
    ]
    height = parts.shape[1]
    for i in range(parts.shape[0]):
        turned[i * height : (i + 1) * height, :] = parts[i]
    first_new, second_new, direction = adam_step(turned[...].T, m[...], v[...])
    m_out[...] = first_new
    v_out[...] = second_new
    copies[0].start()
    copies[1].start()
    product = jnp.zeros(up_out.shape, jnp.float32)
    pieces = []
    for _ in range(3):
        piece = direction.astype(jnp.bfloat16)
        pieces.append(piece)
        direction = direction - piece.astype(jnp.float32)
    for piece in reversed(pieces):
        product += lax.dot_general(
            piece, cols[...], (((1,), (1,)), ((), ())), preferred_element_type=jnp.float32
        )
    up_out[...] = 0.25 * product
    copies[2].start()
    for copy in copies:
        copy.wait()


def last(parts, cols, m, v):
    shape = (CHUNK, RANK)
    out = jax.ShapeDtypeStruct(shape, jnp.float32)
    up = jax.ShapeDtypeStruct((CHUNK, COLS), jnp.float32)
    return pl.pallas_call(
        last_kernel,
        out_shape=(out, out, up),
        in_specs=[VMEM] * 4,
        out_specs=(HBM,) * 3,
        scratch_shapes=[
            pltpu.VMEM((RANK, CHUNK), jnp.float32),
            pltpu.VMEM(shape, jnp.float32),
            pltpu.VMEM(shape, jnp.float32),
            pltpu.VMEM(up.shape, jnp.float32),
            pltpu.SemaphoreType.DMA((3,)),
        ],
        name="last",
    )(*map(in_vmem, (parts, cols, m, v)))


def local(inputs, cotangent, projection_basis, first_moment, second_moment):
    place = jnp.stack([lax.axis_index("fsdp") % 2, lax.axis_index("dp")]).astype(jnp.int32)
    theirs, turned = first(place, inputs, projection_basis, cotangent)
    got = lax.ppermute(theirs, AXES, SWAP)
    mine, cols, m, v = own(
        place, turned, cotangent, projection_basis, first_moment, second_moment
    )
    both = mine + got

    near = exchange(both.reshape(8, ZL // 2, RANK // 4, CHUNK), NEAR)
    near = jnp.sum(near, axis=0).reshape(ZL // 2, 8, RANK // 32, CHUNK)
    far = exchange(near.transpose(1, 0, 2, 3), FAR)
    far = jnp.sum(far, axis=0)
    deep = exchange(jnp.concatenate([far, far], axis=0), DEEP)
    whole = exchange(spread(deep), PLANE)

    return last(whole, cols, m, v)


def solution(mesh):
    in_specs = (
        P(("fsdp", "dp"), None),
        P(("fsdp", "dp"), None),
        P(),
        P("fsdp", None),
        P("fsdp", None),
    )
    out_specs = (P("fsdp", None), P("fsdp", None), P("fsdp", "dp"))
    return jax.shard_map(local, mesh=mesh, in_specs=in_specs, out_specs=out_specs, check_vma=False)
```

```python
import jax
import jax.numpy as jnp
from jax import lax
from jax.experimental import pallas as pl
from jax.experimental.pallas import tpu as pltpu
from jax.sharding import PartitionSpec as P

bias_first = 1.0 - 0.9**10
bias_second = 1.0 - 0.999**10

AXES = ("fsdp", "dp")
X, Y, ZH, ZL = 4, 8, 2, 6
Z = ZH * ZL
IN, OUT, RANK, TOK = 8192, 7680, 128, 128
CHUNK = OUT // (2 * ZL)
COLS = IN // (X * ZH * Y)
KT = 4


def device(x, y, z, core):
    z_hi, z_lo = z // ZL, z % ZL
    return (((z_lo * 2 + core) * X + x) * ZH + z_hi) * Y + y


CORES = (0, 1)


def split(size, core, first, second):
    return tuple(tuple((i + core) % size for i in places) for places in (first, second))


SETS_X = [split(X, c, (1, 2), (0, 3)) for c in CORES]
SETS_Y = [split(Y, c, (1, 2, 4, 7), (0, 3, 5, 6)) for c in CORES]


def pairs(size, core, sets):
    both = [((i + core) % size, (i + core + 1) % size) for i in range(0, size, 2)]
    return [pair if pair[0] in sets[0] else pair[::-1] for pair in both]


EVEN_ODD = (tuple(range(0, Z, 2)), tuple(range(1, Z, 2)))

NEAR = [
    [device(x, y, z, c) for z in pz for x in px for y in py]
    for c in CORES
    for px in pairs(X, c, SETS_X[c])
    for py in pairs(Y, c, SETS_Y[c])
    for pz in pairs(Z, c, EVEN_ODD)
]
FAR = [
    [device(x, y, z, c) for x in xs for y in ys]
    for c in CORES
    for z in range(Z)
    for xs in SETS_X[c]
    for ys in SETS_Y[c]
]
DEEP = [
    [device(x, y, 2 * i + p, c) for i in range(Z // 2)]
    for c in CORES
    for x in range(X)
    for y in range(Y)
    for p in range(2)
]
PLANE = [
    [device(x, y, z, c) for xs in SETS_X[c] for ys in SETS_Y[c] for x in xs for y in ys]
    for c in CORES
    for z in range(Z)
]
SWAP = [
    (device(x, y, z, c), device(x, y, z, 1 - c))
    for x in range(X)
    for y in range(Y)
    for z in range(Z)
    for c in CORES
]


def exchange(blocks, groups):
    return lax.all_to_all(blocks, AXES, 0, 0, axis_index_groups=groups, tiled=True)


def half_copies(c_hbm, c, half, sems):
    def copy(i):
        cols = pl.ds(pl.multiple_of((2 * i + half) * CHUNK, 128), CHUNK)
        return pltpu.make_async_copy(c_hbm.at[:, cols], c.at[i], sems.at[i])

    return [copy(i) for i in range(ZL)]


def half_gradient(turned, c, out):
    for i in range(ZL):
        grad = jnp.dot(turned, c[i], preferred_element_type=jnp.float32)
        out[i % 2, :, i // 2] = grad.reshape(4, RANK // 4, CHUNK)


def first_kernel(x_hbm, b_hbm, c_hbm, out, p_out, x, b, c, xs, bs, cs):
    width = IN // KT

    def x_copy(i):
        part = pl.ds(i * width, width)
        return pltpu.make_async_copy(x_hbm.at[:, part], x.at[:, part], xs.at[i])

    def b_copy(i):
        part = pl.ds(i * width, width)
        return pltpu.make_async_copy(b_hbm.at[part, :], b.at[part, :], bs.at[i])

    for i in range(KT):
        x_copy(i).start()
        b_copy(i).start()
    c_copies = half_copies(c_hbm, c, 1 - lax.axis_index("fsdp") % 2, cs)
    for copy in c_copies:
        copy.start()
    total = jnp.zeros((TOK, RANK), jnp.float32)
    for i in range(KT):
        x_copy(i).wait()
        b_copy(i).wait()
        part = pl.ds(i * width, width)
        total += jnp.dot(x[:, part], b[part, :], preferred_element_type=jnp.float32)
    turned = total.T.astype(jnp.bfloat16)
    p_out[...] = turned
    for copy in c_copies:
        copy.wait()
    half_gradient(turned, c, out)


HALF = (2, 4, ZL // 2, RANK // 4, CHUNK)
VMEM = pl.BlockSpec(memory_space=pltpu.VMEM)
HBM = pl.BlockSpec(memory_space=pltpu.HBM)


def in_hbm(array):
    return pltpu.with_memory_space_constraint(array, pltpu.HBM)


def in_vmem(array):
    return pltpu.with_memory_space_constraint(array, pltpu.VMEM)


def first(inputs, basis, cotangent):
    return pl.pallas_call(
        first_kernel,
        out_shape=(pltpu.VMEM(HALF, jnp.float32), pltpu.VMEM((RANK, TOK), jnp.bfloat16)),
        in_specs=[HBM, HBM, HBM],
        out_specs=(VMEM, VMEM),
        scratch_shapes=[
            pltpu.VMEM((TOK, IN), jnp.bfloat16),
            pltpu.VMEM((IN, RANK), jnp.bfloat16),
            pltpu.VMEM((ZL, TOK, CHUNK), jnp.bfloat16),
            pltpu.SemaphoreType.DMA((KT,)),
            pltpu.SemaphoreType.DMA((KT,)),
            pltpu.SemaphoreType.DMA((ZL,)),
        ],
        compiler_params=pltpu.CompilerParams(vmem_limit_bytes=24 << 20),
        name="first",
    )(*map(in_hbm, (inputs, basis, cotangent)))


def own_kernel(turned, c_hbm, basis_hbm, m_hbm, v_hbm, out, cols, m, v, c, cs, sems):
    rows = pl.ds(pl.multiple_of(lax.axis_index("dp") * COLS, COLS), COLS)
    copies = half_copies(c_hbm, c, lax.axis_index("fsdp") % 2, cs) + [
        pltpu.make_async_copy(basis_hbm.at[rows, :], cols, sems.at[0]),
        pltpu.make_async_copy(m_hbm, m, sems.at[1]),
        pltpu.make_async_copy(v_hbm, v, sems.at[2]),
    ]
    for copy in copies:
        copy.start()
    for copy in copies:
        copy.wait()
    half_gradient(turned[...], c, out)


def own(turned, cotangent, basis, m, v):
    return pl.pallas_call(
        own_kernel,
        out_shape=(
            pltpu.VMEM(HALF, jnp.float32),
            pltpu.VMEM((COLS, RANK), jnp.bfloat16),
            pltpu.VMEM((CHUNK, RANK), jnp.float32),
            pltpu.VMEM((CHUNK, RANK), jnp.float32),
        ),
        in_specs=[VMEM, HBM, HBM, HBM, HBM],
        out_specs=(VMEM,) * 4,
        scratch_shapes=[
            pltpu.VMEM((ZL, TOK, CHUNK), jnp.bfloat16),
            pltpu.SemaphoreType.DMA((ZL,)),
            pltpu.SemaphoreType.DMA((3,)),
        ],
        compiler_params=pltpu.CompilerParams(vmem_limit_bytes=24 << 20),
        cost_estimate=pl.CostEstimate(
            flops=TOK * RANK * OUT, bytes_accessed=TOK * OUT + 2 * RANK * OUT, transcendentals=0
        ),
        name="own",
    )(in_vmem(turned), *map(in_hbm, (cotangent, basis, m, v)))


def adam_step(gradient, first_moment, second_moment):
    first_new = 0.9 * first_moment + 0.1 * gradient
    second_new = 0.999 * second_moment + 0.001 * gradient * gradient
    direction = first_new / bias_first / (jnp.sqrt(second_new / bias_second) + 1e-08)
    return (first_new, second_new, direction)


def spread_kernel(deep, out):
    part = deep[0]
    for i in range(1, deep.shape[0]):
        part += deep[i]
    for i in range(out.shape[0]):
        out[i] = part


def spread(deep):
    return pl.pallas_call(
        spread_kernel,
        out_shape=pltpu.VMEM((X * Y,) + deep.shape[1:], jnp.float32),
        in_specs=[VMEM],
        out_specs=VMEM,
        name="spread",
    )(in_vmem(deep))


def last_kernel(parts, cols, m, v, m_hbm, v_hbm, up_hbm, turned, m_out, v_out, up_out, sems):
    copies = [
        pltpu.make_async_copy(m_out, m_hbm, sems.at[0]),
        pltpu.make_async_copy(v_out, v_hbm, sems.at[1]),
        pltpu.make_async_copy(up_out, up_hbm, sems.at[2]),
    ]
    height = parts.shape[1]
    for i in range(parts.shape[0]):
        turned[i * height : (i + 1) * height, :] = parts[i]
    first_new, second_new, direction = adam_step(turned[...].T, m[...], v[...])
    m_out[...] = first_new
    v_out[...] = second_new
    copies[0].start()
    copies[1].start()
    product = jnp.zeros(up_out.shape, jnp.float32)
    pieces = []
    for _ in range(3):
        piece = direction.astype(jnp.bfloat16)
        pieces.append(piece)
        direction = direction - piece.astype(jnp.float32)
    for piece in reversed(pieces):
        product += lax.dot_general(
            piece, cols[...], (((1,), (1,)), ((), ())), preferred_element_type=jnp.float32
        )
    up_out[...] = 0.25 * product
    copies[2].start()
    for copy in copies:
        copy.wait()


def last(parts, cols, m, v):
    shape = (CHUNK, RANK)
    out = jax.ShapeDtypeStruct(shape, jnp.float32)
    up = jax.ShapeDtypeStruct((CHUNK, COLS), jnp.float32)
    return pl.pallas_call(
        last_kernel,
        out_shape=(out, out, up),
        in_specs=[VMEM] * 4,
        out_specs=(HBM,) * 3,
        scratch_shapes=[
            pltpu.VMEM((RANK, CHUNK), jnp.float32),
            pltpu.VMEM(shape, jnp.float32),
            pltpu.VMEM(shape, jnp.float32),
            pltpu.VMEM(up.shape, jnp.float32),
            pltpu.SemaphoreType.DMA((3,)),
        ],
        name="last",
    )(*map(in_vmem, (parts, cols, m, v)))


def local(inputs, cotangent, projection_basis, first_moment, second_moment):
    theirs, turned = first(inputs, projection_basis, cotangent)
    got = lax.ppermute(theirs, AXES, SWAP)
    mine, cols, m, v = own(
        turned, cotangent, projection_basis, first_moment, second_moment
    )
    both = mine + got

    near = exchange(both.reshape(8, ZL // 2, RANK // 4, CHUNK), NEAR)
    near = jnp.sum(near, axis=0).reshape(ZL // 2, 8, RANK // 32, CHUNK)
    far = exchange(near.transpose(1, 0, 2, 3), FAR)
    far = jnp.sum(far, axis=0)
    deep = exchange(jnp.concatenate([far, far], axis=0), DEEP)
    whole = exchange(spread(deep), PLANE)

    return last(whole, cols, m, v)


def solution(mesh):
    in_specs = (
        P(("fsdp", "dp"), None),
        P(("fsdp", "dp"), None),
        P(),
        P("fsdp", None),
        P("fsdp", None),
    )
    out_specs = (P("fsdp", None), P("fsdp", None), P("fsdp", "dp"))
    return jax.shard_map(local, mesh=mesh, in_specs=in_specs, out_specs=out_specs, check_vma=False)
```

```python
import jax
import jax.numpy as jnp
from jax import lax
from jax.experimental import pallas as pl
from jax.experimental.pallas import tpu as pltpu
from jax.sharding import PartitionSpec as P

bias_first = 1.0 - 0.9**10
bias_second = 1.0 - 0.999**10

AXES = ("fsdp", "dp")
X, Y, ZH, ZL = 4, 8, 2, 6
Z = ZH * ZL
IN, OUT, RANK, TOK = 8192, 7680, 128, 128
CHUNK = OUT // (2 * ZL)
COLS = IN // (X * ZH * Y)
KT = 4


def device(x, y, z, core):
    z_hi, z_lo = z // ZL, z % ZL
    return (((z_lo * 2 + core) * X + x) * ZH + z_hi) * Y + y


CORES = (0, 1)


def split(size, core, first, second):
    return tuple(tuple((i + core) % size for i in places) for places in (first, second))


SETS_X = [split(X, c, (1, 2), (0, 3)) for c in CORES]
SETS_Y = [split(Y, c, (1, 2, 4, 7), (0, 3, 5, 6)) for c in CORES]


def pairs(size, core, sets):
    both = [((i + core) % size, (i + core + 1) % size) for i in range(0, size, 2)]
    return [pair if pair[0] in sets[0] else pair[::-1] for pair in both]


EVEN_ODD = (tuple(range(0, Z, 2)), tuple(range(1, Z, 2)))

NEAR = [
    [device(x, y, z, c) for z in pz for x in px for y in py]
    for c in CORES
    for px in pairs(X, c, SETS_X[c])
    for py in pairs(Y, c, SETS_Y[c])
    for pz in pairs(Z, 1 - c, EVEN_ODD)
]
FAR = [
    [device(x, y, z, c) for x in xs for y in ys]
    for c in CORES
    for z in range(Z)
    for xs in SETS_X[c]
    for ys in SETS_Y[c]
]
DEEP = [
    [device(x, y, 2 * i + p, c) for i in range(Z // 2)]
    for c in CORES
    for x in range(X)
    for y in range(Y)
    for p in range(2)
]
PLANE = [
    [device(x, y, z, c) for xs in SETS_X[c] for ys in SETS_Y[c] for x in xs for y in ys]
    for c in CORES
    for z in range(Z)
]
SWAP = [
    (device(x, y, z, c), device(x, y, z, 1 - c))
    for x in range(X)
    for y in range(Y)
    for z in range(Z)
    for c in CORES
]


def exchange(blocks, groups):
    return lax.all_to_all(blocks, AXES, 0, 0, axis_index_groups=groups, tiled=True)


def half_copies(c_hbm, c, half, sems):
    def copy(i):
        cols = pl.ds(pl.multiple_of((2 * i + half) * CHUNK, 128), CHUNK)
        return pltpu.make_async_copy(c_hbm.at[:, cols], c.at[i], sems.at[i])

    return [copy(i) for i in range(ZL)]


def half_gradient(turned, c, out):
    for i in range(ZL):
        grad = jnp.dot(turned, c[i], preferred_element_type=jnp.float32)
        out[i % 2, :, i // 2] = grad.reshape(4, RANK // 4, CHUNK)


def first_kernel(x_hbm, b_hbm, c_hbm, out, p_out, x, b, c, xs, bs, cs):
    width = IN // KT

    def x_copy(i):
        part = pl.ds(i * width, width)
        return pltpu.make_async_copy(x_hbm.at[:, part], x.at[:, part], xs.at[i])

    def b_copy(i):
        part = pl.ds(i * width, width)
        return pltpu.make_async_copy(b_hbm.at[part, :], b.at[part, :], bs.at[i])

    for i in range(KT):
        x_copy(i).start()
        b_copy(i).start()
    c_copies = half_copies(c_hbm, c, 1 - lax.axis_index("fsdp") % 2, cs)
    for copy in c_copies:
        copy.start()
    total = jnp.zeros((TOK, RANK), jnp.float32)
    for i in range(KT):
        x_copy(i).wait()
        b_copy(i).wait()
        part = pl.ds(i * width, width)
        total += jnp.dot(x[:, part], b[part, :], preferred_element_type=jnp.float32)
    turned = total.T.astype(jnp.bfloat16)
    p_out[...] = turned
    for copy in c_copies:
        copy.wait()
    half_gradient(turned, c, out)


HALF = (2, 4, ZL // 2, RANK // 4, CHUNK)
VMEM = pl.BlockSpec(memory_space=pltpu.VMEM)
HBM = pl.BlockSpec(memory_space=pltpu.HBM)


def in_hbm(array):
    return pltpu.with_memory_space_constraint(array, pltpu.HBM)


def in_vmem(array):
    return pltpu.with_memory_space_constraint(array, pltpu.VMEM)


def first(inputs, basis, cotangent):
    return pl.pallas_call(
        first_kernel,
        out_shape=(pltpu.VMEM(HALF, jnp.float32), pltpu.VMEM((RANK, TOK), jnp.bfloat16)),
        in_specs=[HBM, HBM, HBM],
        out_specs=(VMEM, VMEM),
        scratch_shapes=[
            pltpu.VMEM((TOK, IN), jnp.bfloat16),
            pltpu.VMEM((IN, RANK), jnp.bfloat16),
            pltpu.VMEM((ZL, TOK, CHUNK), jnp.bfloat16),
            pltpu.SemaphoreType.DMA((KT,)),
            pltpu.SemaphoreType.DMA((KT,)),
            pltpu.SemaphoreType.DMA((ZL,)),
        ],
        compiler_params=pltpu.CompilerParams(vmem_limit_bytes=24 << 20),
        name="first",
    )(*map(in_hbm, (inputs, basis, cotangent)))


def own_kernel(turned, c_hbm, basis_hbm, m_hbm, v_hbm, out, cols, m, v, c, cs, sems):
    rows = pl.ds(pl.multiple_of(lax.axis_index("dp") * COLS, COLS), COLS)
    copies = half_copies(c_hbm, c, lax.axis_index("fsdp") % 2, cs) + [
        pltpu.make_async_copy(basis_hbm.at[rows, :], cols, sems.at[0]),
        pltpu.make_async_copy(m_hbm, m, sems.at[1]),
        pltpu.make_async_copy(v_hbm, v, sems.at[2]),
    ]
    for copy in copies:
        copy.start()
    for copy in copies:
        copy.wait()
    half_gradient(turned[...], c, out)


def own(turned, cotangent, basis, m, v):
    return pl.pallas_call(
        own_kernel,
        out_shape=(
            pltpu.VMEM(HALF, jnp.float32),
            pltpu.VMEM((COLS, RANK), jnp.bfloat16),
            pltpu.VMEM((CHUNK, RANK), jnp.float32),
            pltpu.VMEM((CHUNK, RANK), jnp.float32),
        ),
        in_specs=[VMEM, HBM, HBM, HBM, HBM],
        out_specs=(VMEM,) * 4,
        scratch_shapes=[
            pltpu.VMEM((ZL, TOK, CHUNK), jnp.bfloat16),
            pltpu.SemaphoreType.DMA((ZL,)),
            pltpu.SemaphoreType.DMA((3,)),
        ],
        compiler_params=pltpu.CompilerParams(vmem_limit_bytes=24 << 20),
        cost_estimate=pl.CostEstimate(
            flops=TOK * RANK * OUT, bytes_accessed=TOK * OUT + 2 * RANK * OUT, transcendentals=0
        ),
        name="own",
    )(in_vmem(turned), *map(in_hbm, (cotangent, basis, m, v)))


def adam_step(gradient, first_moment, second_moment):
    first_new = 0.9 * first_moment + 0.1 * gradient
    second_new = 0.999 * second_moment + 0.001 * gradient * gradient
    direction = first_new / bias_first / (jnp.sqrt(second_new / bias_second) + 1e-08)
    return (first_new, second_new, direction)


def settle_kernel(near, out):
    for k in range(near.shape[1]):
        total = near[0, k]
        for i in range(1, near.shape[0]):
            total += near[i, k]
        height = out.shape[2]
        for r in range(out.shape[0]):
            out[r, k] = total[r * height : (r + 1) * height]


def settle(near):
    _, chunks, rows, width = near.shape
    return pl.pallas_call(
        settle_kernel,
        out_shape=pltpu.VMEM((8, chunks, rows // 8, width), jnp.float32),
        in_specs=[VMEM],
        out_specs=VMEM,
        name="settle",
    )(in_vmem(near))


def twice_kernel(far, out):
    for k in range(far.shape[1]):
        total = far[0, k]
        for i in range(1, far.shape[0]):
            total += far[i, k]
        for h in range(ZH):
            out[h * ZL // 2 + k] = total


def twice(far):
    return pl.pallas_call(
        twice_kernel,
        out_shape=pltpu.VMEM((Z // 2,) + far.shape[2:], jnp.float32),
        in_specs=[VMEM],
        out_specs=VMEM,
        name="twice",
    )(in_vmem(far))


def spread_kernel(deep, out):
    part = deep[0]
    for i in range(1, deep.shape[0]):
        part += deep[i]
    for i in range(out.shape[0]):
        out[i] = part


def spread(deep):
    return pl.pallas_call(
        spread_kernel,
        out_shape=pltpu.VMEM((X * Y,) + deep.shape[1:], jnp.float32),
        in_specs=[VMEM],
        out_specs=VMEM,
        name="spread",
    )(in_vmem(deep))


def last_kernel(parts, cols, m, v, m_hbm, v_hbm, up_hbm, turned, m_out, v_out, up_out, sems):
    copies = [
        pltpu.make_async_copy(m_out, m_hbm, sems.at[0]),
        pltpu.make_async_copy(v_out, v_hbm, sems.at[1]),
        pltpu.make_async_copy(up_out, up_hbm, sems.at[2]),
    ]
    height = parts.shape[1]
    for i in range(parts.shape[0]):
        turned[i * height : (i + 1) * height, :] = parts[i]
    first_new, second_new, direction = adam_step(turned[...].T, m[...], v[...])
    m_out[...] = first_new
    v_out[...] = second_new
    copies[0].start()
    copies[1].start()
    product = jnp.zeros(up_out.shape, jnp.float32)
    pieces = []
    for _ in range(3):
        piece = direction.astype(jnp.bfloat16)
        pieces.append(piece)
        direction = direction - piece.astype(jnp.float32)
    for piece in reversed(pieces):
        product += lax.dot_general(
            piece, cols[...], (((1,), (1,)), ((), ())), preferred_element_type=jnp.float32
        )
    up_out[...] = 0.25 * product
    copies[2].start()
    for copy in copies:
        copy.wait()


def last(parts, cols, m, v):
    shape = (CHUNK, RANK)
    out = jax.ShapeDtypeStruct(shape, jnp.float32)
    up = jax.ShapeDtypeStruct((CHUNK, COLS), jnp.float32)
    return pl.pallas_call(
        last_kernel,
        out_shape=(out, out, up),
        in_specs=[VMEM] * 4,
        out_specs=(HBM,) * 3,
        scratch_shapes=[
            pltpu.VMEM((RANK, CHUNK), jnp.float32),
            pltpu.VMEM(shape, jnp.float32),
            pltpu.VMEM(shape, jnp.float32),
            pltpu.VMEM(up.shape, jnp.float32),
            pltpu.SemaphoreType.DMA((3,)),
        ],
        name="last",
    )(*map(in_vmem, (parts, cols, m, v)))


def local(inputs, cotangent, projection_basis, first_moment, second_moment):
    theirs, turned = first(inputs, projection_basis, cotangent)
    got = lax.ppermute(theirs, AXES, SWAP)
    mine, cols, m, v = own(
        turned, cotangent, projection_basis, first_moment, second_moment
    )
    both = mine + got

    near = exchange(both.reshape(8, ZL // 2, RANK // 4, CHUNK), NEAR)
    far = exchange(settle(near), FAR)
    deep = exchange(twice(far), DEEP)
    whole = exchange(spread(deep), PLANE)

    return last(whole, cols, m, v)


def solution(mesh):
    in_specs = (
        P(("fsdp", "dp"), None),
        P(("fsdp", "dp"), None),
        P(),
        P("fsdp", None),
        P("fsdp", None),
    )
    out_specs = (P("fsdp", None), P("fsdp", None), P("fsdp", "dp"))
    return jax.shard_map(local, mesh=mesh, in_specs=in_specs, out_specs=out_specs, check_vma=False)
```

```python
import jax
import jax.numpy as jnp
from jax import lax
from jax.experimental import pallas as pl
from jax.experimental.pallas import tpu as pltpu
from jax.sharding import PartitionSpec as P

bias_first = 1.0 - 0.9**10
bias_second = 1.0 - 0.999**10

AXES = ("fsdp", "dp")
X, Y, ZH, ZL = 4, 8, 2, 6
Z = ZH * ZL
IN, OUT, RANK, TOK = 8192, 7680, 128, 128
CHUNK = OUT // (2 * ZL)
COLS = IN // (X * ZH * Y)
KT = 4


def device(x, y, z, core):
    z_hi, z_lo = z // ZL, z % ZL
    return (((z_lo * 2 + core) * X + x) * ZH + z_hi) * Y + y


CORES = (0, 1)


def split(size, core, first, second):
    return tuple(tuple((i + core) % size for i in places) for places in (first, second))


SETS_X = [((0, 2), (1, 3)), split(X, 1, (1, 2), (0, 3))]
SETS_Y = [split(Y, c, (1, 2, 4, 7), (0, 3, 5, 6)) for c in CORES]


def pairs(size, core, sets):
    both = [((i + core) % size, (i + core + 1) % size) for i in range(0, size, 2)]
    return [pair if pair[0] in sets[0] else pair[::-1] for pair in both]


EVEN_ODD = (tuple(range(0, Z, 2)), tuple(range(1, Z, 2)))

NEAR = [
    [device(x, y, z, c) for z in pz for x in px for y in py]
    for c in CORES
    for px in pairs(X, c, SETS_X[c])
    for py in pairs(Y, c, SETS_Y[c])
    for pz in pairs(Z, 1 - c, EVEN_ODD)
]
FAR = [
    [device(x, y, z, c) for x in xs for y in ys]
    for c in CORES
    for z in range(Z)
    for xs in SETS_X[c]
    for ys in SETS_Y[c]
]
DEEP = [
    [device(x, y, 2 * i + p, c) for i in range(Z // 2)]
    for c in CORES
    for x in range(X)
    for y in range(Y)
    for p in range(2)
]
PLANE = [
    [device(x, y, z, c) for xs in SETS_X[c] for ys in SETS_Y[c] for x in xs for y in ys]
    for c in CORES
    for z in range(Z)
]
SWAP = [
    (device(x, y, z, c), device(x, y, z, 1 - c))
    for x in range(X)
    for y in range(Y)
    for z in range(Z)
    for c in CORES
]


def exchange(blocks, groups):
    return lax.all_to_all(blocks, AXES, 0, 0, axis_index_groups=groups, tiled=True)


def half_copies(c_hbm, c, half, sems):
    def copy(i):
        cols = pl.ds(pl.multiple_of((2 * i + half) * CHUNK, 128), CHUNK)
        return pltpu.make_async_copy(c_hbm.at[:, cols], c.at[i], sems.at[i])

    return [copy(i) for i in range(ZL)]


def half_gradient(turned, c, out):
    for i in range(ZL):
        grad = jnp.dot(turned, c[i], preferred_element_type=jnp.float32)
        out[i % 2, :, i // 2] = grad.reshape(4, RANK // 4, CHUNK)


def first_kernel(x_hbm, b_hbm, c_hbm, out, p_out, x, b, c, xs, bs, cs):
    width = IN // KT

    def x_copy(i):
        part = pl.ds(i * width, width)
        return pltpu.make_async_copy(x_hbm.at[:, part], x.at[:, part], xs.at[i])

    def b_copy(i):
        part = pl.ds(i * width, width)
        return pltpu.make_async_copy(b_hbm.at[part, :], b.at[part, :], bs.at[i])

    for i in range(KT):
        x_copy(i).start()
        b_copy(i).start()
    c_copies = half_copies(c_hbm, c, 1 - lax.axis_index("fsdp") % 2, cs)
    for copy in c_copies:
        copy.start()
    total = jnp.zeros((TOK, RANK), jnp.float32)
    for i in range(KT):
        x_copy(i).wait()
        b_copy(i).wait()
        part = pl.ds(i * width, width)
        total += jnp.dot(x[:, part], b[part, :], preferred_element_type=jnp.float32)
    turned = total.T.astype(jnp.bfloat16)
    p_out[...] = turned
    for copy in c_copies:
        copy.wait()
    half_gradient(turned, c, out)


HALF = (2, 4, ZL // 2, RANK // 4, CHUNK)
VMEM = pl.BlockSpec(memory_space=pltpu.VMEM)
HBM = pl.BlockSpec(memory_space=pltpu.HBM)


def in_hbm(array):
    return pltpu.with_memory_space_constraint(array, pltpu.HBM)


def in_vmem(array):
    return pltpu.with_memory_space_constraint(array, pltpu.VMEM)


def first(inputs, basis, cotangent):
    return pl.pallas_call(
        first_kernel,
        out_shape=(pltpu.VMEM(HALF, jnp.float32), pltpu.VMEM((RANK, TOK), jnp.bfloat16)),
        in_specs=[HBM, HBM, HBM],
        out_specs=(VMEM, VMEM),
        scratch_shapes=[
            pltpu.VMEM((TOK, IN), jnp.bfloat16),
            pltpu.VMEM((IN, RANK), jnp.bfloat16),
            pltpu.VMEM((ZL, TOK, CHUNK), jnp.bfloat16),
            pltpu.SemaphoreType.DMA((KT,)),
            pltpu.SemaphoreType.DMA((KT,)),
            pltpu.SemaphoreType.DMA((ZL,)),
        ],
        compiler_params=pltpu.CompilerParams(vmem_limit_bytes=24 << 20),
        name="first",
    )(*map(in_hbm, (inputs, basis, cotangent)))


def own_kernel(turned, c_hbm, basis_hbm, m_hbm, v_hbm, out, cols, m, v, c, cs, sems):
    rows = pl.ds(pl.multiple_of(lax.axis_index("dp") * COLS, COLS), COLS)
    copies = half_copies(c_hbm, c, lax.axis_index("fsdp") % 2, cs) + [
        pltpu.make_async_copy(basis_hbm.at[rows, :], cols, sems.at[0]),
        pltpu.make_async_copy(m_hbm, m, sems.at[1]),
        pltpu.make_async_copy(v_hbm, v, sems.at[2]),
    ]
    for copy in copies:
        copy.start()
    for copy in copies:
        copy.wait()
    half_gradient(turned[...], c, out)


def own(turned, cotangent, basis, m, v):
    return pl.pallas_call(
        own_kernel,
        out_shape=(
            pltpu.VMEM(HALF, jnp.float32),
            pltpu.VMEM((COLS, RANK), jnp.bfloat16),
            pltpu.VMEM((CHUNK, RANK), jnp.float32),
            pltpu.VMEM((CHUNK, RANK), jnp.float32),
        ),
        in_specs=[VMEM, HBM, HBM, HBM, HBM],
        out_specs=(VMEM,) * 4,
        scratch_shapes=[
            pltpu.VMEM((ZL, TOK, CHUNK), jnp.bfloat16),
            pltpu.SemaphoreType.DMA((ZL,)),
            pltpu.SemaphoreType.DMA((3,)),
        ],
        compiler_params=pltpu.CompilerParams(vmem_limit_bytes=24 << 20),
        cost_estimate=pl.CostEstimate(
            flops=TOK * RANK * OUT, bytes_accessed=TOK * OUT + 2 * RANK * OUT, transcendentals=0
        ),
        name="own",
    )(in_vmem(turned), *map(in_hbm, (cotangent, basis, m, v)))


def adam_step(gradient, first_moment, second_moment):
    first_new = 0.9 * first_moment + 0.1 * gradient
    second_new = 0.999 * second_moment + 0.001 * gradient * gradient
    direction = first_new / bias_first / (jnp.sqrt(second_new / bias_second) + 1e-08)
    return (first_new, second_new, direction)


def settle_kernel(near, out):
    for k in range(near.shape[1]):
        total = near[0, k]
        for i in range(1, near.shape[0]):
            total += near[i, k]
        height = out.shape[2]
        for r in range(out.shape[0]):
            out[r, k] = total[r * height : (r + 1) * height]


def settle(near):
    _, chunks, rows, width = near.shape
    return pl.pallas_call(
        settle_kernel,
        out_shape=pltpu.VMEM((8, chunks, rows // 8, width), jnp.float32),
        in_specs=[VMEM],
        out_specs=VMEM,
        name="settle",
    )(in_vmem(near))


def twice_kernel(far, out):
    for k in range(far.shape[1]):
        total = far[0, k]
        for i in range(1, far.shape[0]):
            total += far[i, k]
        for h in range(ZH):
            out[h * ZL // 2 + k] = total


def twice(far):
    return pl.pallas_call(
        twice_kernel,
        out_shape=pltpu.VMEM((Z // 2,) + far.shape[2:], jnp.float32),
        in_specs=[VMEM],
        out_specs=VMEM,
        name="twice",
    )(in_vmem(far))


def spread_kernel(deep, out):
    part = deep[0]
    for i in range(1, deep.shape[0]):
        part += deep[i]
    for i in range(out.shape[0]):
        out[i] = part


def spread(deep):
    return pl.pallas_call(
        spread_kernel,
        out_shape=pltpu.VMEM((X * Y,) + deep.shape[1:], jnp.float32),
        in_specs=[VMEM],
        out_specs=VMEM,
        name="spread",
    )(in_vmem(deep))


def last_kernel(parts, cols, m, v, m_hbm, v_hbm, up_hbm, turned, m_out, v_out, up_out, sems):
    copies = [
        pltpu.make_async_copy(m_out, m_hbm, sems.at[0]),
        pltpu.make_async_copy(v_out, v_hbm, sems.at[1]),
        pltpu.make_async_copy(up_out, up_hbm, sems.at[2]),
    ]
    height = parts.shape[1]
    for i in range(parts.shape[0]):
        turned[i * height : (i + 1) * height, :] = parts[i]
    first_new, second_new, direction = adam_step(turned[...].T, m[...], v[...])
    m_out[...] = first_new
    v_out[...] = second_new
    copies[0].start()
    copies[1].start()
    product = jnp.zeros(up_out.shape, jnp.float32)
    pieces = []
    for _ in range(3):
        piece = direction.astype(jnp.bfloat16)
        pieces.append(piece)
        direction = direction - piece.astype(jnp.float32)
    for piece in reversed(pieces):
        product += lax.dot_general(
            piece, cols[...], (((1,), (1,)), ((), ())), preferred_element_type=jnp.float32
        )
    up_out[...] = 0.25 * product
    copies[2].start()
    for copy in copies:
        copy.wait()


def last(parts, cols, m, v):
    shape = (CHUNK, RANK)
    out = jax.ShapeDtypeStruct(shape, jnp.float32)
    up = jax.ShapeDtypeStruct((CHUNK, COLS), jnp.float32)
    return pl.pallas_call(
        last_kernel,
        out_shape=(out, out, up),
        in_specs=[VMEM] * 4,
        out_specs=(HBM,) * 3,
        scratch_shapes=[
            pltpu.VMEM((RANK, CHUNK), jnp.float32),
            pltpu.VMEM(shape, jnp.float32),
            pltpu.VMEM(shape, jnp.float32),
            pltpu.VMEM(up.shape, jnp.float32),
            pltpu.SemaphoreType.DMA((3,)),
        ],
        name="last",
    )(*map(in_vmem, (parts, cols, m, v)))


def local(inputs, cotangent, projection_basis, first_moment, second_moment):
    theirs, turned = first(inputs, projection_basis, cotangent)
    got = lax.ppermute(theirs, AXES, SWAP)
    mine, cols, m, v = own(
        turned, cotangent, projection_basis, first_moment, second_moment
    )
    both = mine + got

    near = exchange(both.reshape(8, ZL // 2, RANK // 4, CHUNK), NEAR)
    far = exchange(settle(near), FAR)
    deep = exchange(twice(far), DEEP)
    whole = exchange(spread(deep), PLANE)

    return last(whole, cols, m, v)


def solution(mesh):
    in_specs = (
        P(("fsdp", "dp"), None),
        P(("fsdp", "dp"), None),
        P(),
        P("fsdp", None),
        P("fsdp", None),
    )
    out_specs = (P("fsdp", None), P("fsdp", None), P("fsdp", "dp"))
    return jax.shard_map(local, mesh=mesh, in_specs=in_specs, out_specs=out_specs, check_vma=False)
```

```python
import jax
import jax.numpy as jnp
from jax import lax
from jax.experimental import pallas as pl
from jax.experimental.pallas import tpu as pltpu
from jax.sharding import PartitionSpec as P

bias_first = 1.0 - 0.9**10
bias_second = 1.0 - 0.999**10

AXES = ("fsdp", "dp")
X, Y, ZH, ZL = 4, 8, 2, 6
Z = ZH * ZL
IN, OUT, RANK, TOK = 8192, 7680, 128, 128
CHUNK = OUT // (2 * ZL)
COLS = IN // (X * ZH * Y)
KT = 4


def device(x, y, z, core):
    z_hi, z_lo = z // ZL, z % ZL
    return (((z_lo * 2 + core) * X + x) * ZH + z_hi) * Y + y


CORES = (0, 1)


def split(size, core, first, second):
    return tuple(tuple((i + core) % size for i in places) for places in (first, second))


SETS_X = [split(X, c, (1, 2), (0, 3)) for c in CORES]
SETS_Y = [split(Y, c, (1, 2, 4, 7), (0, 3, 5, 6)) for c in CORES]


def pairs(size, core, sets):
    both = [((i + core) % size, (i + core + 1) % size) for i in range(0, size, 2)]
    return [pair if pair[0] in sets[0] else pair[::-1] for pair in both]


EVEN_ODD = (tuple(range(0, Z, 2)), tuple(range(1, Z, 2)))

NEAR = [
    [device(x, y, z, c) for z in pz for x in px for y in py]
    for c in CORES
    for px in pairs(X, c, SETS_X[c])
    for py in pairs(Y, c, SETS_Y[c])
    for pz in pairs(Z, c, EVEN_ODD)
]
FAR = [
    [device(x, y, z, c) for x in xs for y in ys]
    for c in CORES
    for z in range(Z)
    for xs in SETS_X[c]
    for ys in SETS_Y[c]
]
DEEP = [
    [device(x, y, 2 * i + p, c) for i in range(Z // 2)]
    for c in CORES
    for x in range(X)
    for y in range(Y)
    for p in range(2)
]
PLANE = [
    [device(x, y, z, c) for xs in SETS_X[c] for ys in SETS_Y[c] for x in xs for y in ys]
    for c in CORES
    for z in range(Z)
]
SWAP = [
    (device(x, y, z, c), device(x, y, z, 1 - c))
    for x in range(X)
    for y in range(Y)
    for z in range(Z)
    for c in CORES
]


def exchange(blocks, groups):
    return lax.all_to_all(blocks, AXES, 0, 0, axis_index_groups=groups, tiled=True)


def half_copies(c_hbm, c, half, sems):
    def copy(i):
        cols = pl.ds(pl.multiple_of((2 * i + half) * CHUNK, 128), CHUNK)
        return pltpu.make_async_copy(c_hbm.at[:, cols], c.at[i], sems.at[i])

    return [copy(i) for i in range(ZL)]


def half_gradient(turned, c, out):
    for i in range(ZL):
        grad = jnp.dot(turned, c[i], preferred_element_type=jnp.float32)
        out[i % 2, :, i // 2] = grad.reshape(4, RANK // 4, CHUNK)


def first_kernel(x_hbm, b_hbm, c_hbm, out, p_out, x, b, c, xs, bs, cs):
    width = IN // KT

    def x_copy(i):
        part = pl.ds(i * width, width)
        return pltpu.make_async_copy(x_hbm.at[:, part], x.at[:, part], xs.at[i])

    def b_copy(i):
        part = pl.ds(i * width, width)
        return pltpu.make_async_copy(b_hbm.at[part, :], b.at[part, :], bs.at[i])

    for i in range(KT):
        x_copy(i).start()
        b_copy(i).start()
    c_copies = half_copies(c_hbm, c, 1 - lax.axis_index("fsdp") % 2, cs)
    for copy in c_copies:
        copy.start()
    total = jnp.zeros((TOK, RANK), jnp.float32)
    for i in range(KT):
        x_copy(i).wait()
        b_copy(i).wait()
        part = pl.ds(i * width, width)
        total += jnp.dot(x[:, part], b[part, :], preferred_element_type=jnp.float32)
    turned = total.T.astype(jnp.bfloat16)
    p_out[...] = turned
    for copy in c_copies:
        copy.wait()
    half_gradient(turned, c, out)


HALF = (2, 4, ZL // 2, RANK // 4, CHUNK)
VMEM = pl.BlockSpec(memory_space=pltpu.VMEM)
HBM = pl.BlockSpec(memory_space=pltpu.HBM)


def in_hbm(array):
    return pltpu.with_memory_space_constraint(array, pltpu.HBM)


def in_vmem(array):
    return pltpu.with_memory_space_constraint(array, pltpu.VMEM)


def first(inputs, basis, cotangent):
    return pl.pallas_call(
        first_kernel,
        out_shape=(pltpu.VMEM(HALF, jnp.float32), pltpu.VMEM((RANK, TOK), jnp.bfloat16)),
        in_specs=[HBM, HBM, HBM],
        out_specs=(VMEM, VMEM),
        scratch_shapes=[
            pltpu.VMEM((TOK, IN), jnp.bfloat16),
            pltpu.VMEM((IN, RANK), jnp.bfloat16),
            pltpu.VMEM((ZL, TOK, CHUNK), jnp.bfloat16),
            pltpu.SemaphoreType.DMA((KT,)),
            pltpu.SemaphoreType.DMA((KT,)),
            pltpu.SemaphoreType.DMA((ZL,)),
        ],
        compiler_params=pltpu.CompilerParams(vmem_limit_bytes=24 << 20),
        name="first",
    )(*map(in_hbm, (inputs, basis, cotangent)))


def own_kernel(turned, c_hbm, basis_hbm, m_hbm, v_hbm, out, cols, m, v, c, cs, sems):
    rows = pl.ds(pl.multiple_of(lax.axis_index("dp") * COLS, COLS), COLS)
    copies = half_copies(c_hbm, c, lax.axis_index("fsdp") % 2, cs) + [
        pltpu.make_async_copy(basis_hbm.at[rows, :], cols, sems.at[0]),
        pltpu.make_async_copy(m_hbm, m, sems.at[1]),
        pltpu.make_async_copy(v_hbm, v, sems.at[2]),
    ]
    for copy in copies:
        copy.start()
    for copy in copies:
        copy.wait()
    half_gradient(turned[...], c, out)


def own(turned, cotangent, basis, m, v):
    return pl.pallas_call(
        own_kernel,
        out_shape=(
            pltpu.VMEM(HALF, jnp.float32),
            pltpu.VMEM((COLS, RANK), jnp.bfloat16),
            pltpu.VMEM((CHUNK, RANK), jnp.float32),
            pltpu.VMEM((CHUNK, RANK), jnp.float32),
        ),
        in_specs=[VMEM, HBM, HBM, HBM, HBM],
        out_specs=(VMEM,) * 4,
        scratch_shapes=[
            pltpu.VMEM((ZL, TOK, CHUNK), jnp.bfloat16),
            pltpu.SemaphoreType.DMA((ZL,)),
            pltpu.SemaphoreType.DMA((3,)),
        ],
        compiler_params=pltpu.CompilerParams(vmem_limit_bytes=24 << 20),
        cost_estimate=pl.CostEstimate(
            flops=TOK * RANK * OUT, bytes_accessed=TOK * OUT + 2 * RANK * OUT, transcendentals=0
        ),
        name="own",
    )(in_vmem(turned), *map(in_hbm, (cotangent, basis, m, v)))


def adam_step(gradient, first_moment, second_moment):
    first_new = 0.9 * first_moment + 0.1 * gradient
    second_new = 0.999 * second_moment + 0.001 * gradient * gradient
    direction = first_new / bias_first / (jnp.sqrt(second_new / bias_second) + 1e-08)
    return (first_new, second_new, direction)


def settle_kernel(near, out):
    for k in range(near.shape[1]):
        total = near[0, k]
        for i in range(1, near.shape[0]):
            total += near[i, k]
        height = out.shape[2]
        for r in range(out.shape[0]):
            out[r, k] = total[r * height : (r + 1) * height]


def settle(near):
    _, chunks, rows, width = near.shape
    return pl.pallas_call(
        settle_kernel,
        out_shape=pltpu.VMEM((8, chunks, rows // 8, width), jnp.float32),
        in_specs=[VMEM],
        out_specs=VMEM,
        name="settle",
    )(in_vmem(near))


def twice_kernel(far, out):
    for k in range(far.shape[1]):
        total = far[0, k]
        for i in range(1, far.shape[0]):
            total += far[i, k]
        for h in range(ZH):
            out[h * ZL // 2 + k] = total


def twice(far):
    return pl.pallas_call(
        twice_kernel,
        out_shape=pltpu.VMEM((Z // 2,) + far.shape[2:], jnp.float32),
        in_specs=[VMEM],
        out_specs=VMEM,
        name="twice",
    )(in_vmem(far))


def spread_kernel(deep, out):
    part = deep[0]
    for i in range(1, deep.shape[0]):
        part += deep[i]
    for i in range(out.shape[0]):
        out[i] = part


def spread(deep):
    return pl.pallas_call(
        spread_kernel,
        out_shape=pltpu.VMEM((X * Y,) + deep.shape[1:], jnp.float32),
        in_specs=[VMEM],
        out_specs=VMEM,
        name="spread",
    )(in_vmem(deep))


def last_kernel(parts, cols, m, v, m_hbm, v_hbm, up_hbm, turned, m_out, v_out, up_out, sems):
    copies = [
        pltpu.make_async_copy(m_out, m_hbm, sems.at[0]),
        pltpu.make_async_copy(v_out, v_hbm, sems.at[1]),
        pltpu.make_async_copy(up_out, up_hbm, sems.at[2]),
    ]
    height = parts.shape[1]
    for i in range(parts.shape[0]):
        turned[i * height : (i + 1) * height, :] = parts[i]
    first_new, second_new, direction = adam_step(turned[...].T, m[...], v[...])
    m_out[...] = first_new
    v_out[...] = second_new
    copies[0].start()
    copies[1].start()
    product = jnp.zeros(up_out.shape, jnp.float32)
    pieces = []
    for _ in range(3):
        piece = direction.astype(jnp.bfloat16)
        pieces.append(piece)
        direction = direction - piece.astype(jnp.float32)
    for piece in reversed(pieces):
        product += lax.dot_general(
            piece, cols[...], (((1,), (1,)), ((), ())), preferred_element_type=jnp.float32
        )
    up_out[...] = 0.25 * product
    copies[2].start()
    for copy in copies:
        copy.wait()


def last(parts, cols, m, v):
    shape = (CHUNK, RANK)
    out = jax.ShapeDtypeStruct(shape, jnp.float32)
    up = jax.ShapeDtypeStruct((CHUNK, COLS), jnp.float32)
    return pl.pallas_call(
        last_kernel,
        out_shape=(out, out, up),
        in_specs=[VMEM] * 4,
        out_specs=(HBM,) * 3,
        scratch_shapes=[
            pltpu.VMEM((RANK, CHUNK), jnp.float32),
            pltpu.VMEM(shape, jnp.float32),
            pltpu.VMEM(shape, jnp.float32),
            pltpu.VMEM(up.shape, jnp.float32),
            pltpu.SemaphoreType.DMA((3,)),
        ],
        name="last",
    )(*map(in_vmem, (parts, cols, m, v)))


def local(inputs, cotangent, projection_basis, first_moment, second_moment):
    theirs, turned = first(inputs, projection_basis, cotangent)
    got = lax.ppermute(theirs, AXES, SWAP)
    mine, cols, m, v = own(
        turned, cotangent, projection_basis, first_moment, second_moment
    )
    both = mine + got

    near = exchange(both.reshape(8, ZL // 2, RANK // 4, CHUNK), NEAR)
    far = exchange(settle(near), FAR)
    deep = exchange(twice(far), DEEP)
    whole = exchange(spread(deep), PLANE)

    return last(whole, cols, m, v)


def solution(mesh):
    in_specs = (
        P(("fsdp", "dp"), None),
        P(("fsdp", "dp"), None),
        P(),
        P("fsdp", None),
        P("fsdp", None),
    )
    out_specs = (P("fsdp", None), P("fsdp", None), P("fsdp", "dp"))
    return jax.shard_map(local, mesh=mesh, in_specs=in_specs, out_specs=out_specs, check_vma=False)
```
